32 devices in a mesh: groups: 2 (over x), tokens: 16 (over z, y, core).
Axes of the slice: x: 2, y: 2, z: 4, core: 2. Of those that a mesh axis runs over, the one named last changes fastest.
Arguments:
- queries: bfloat16 [4096, 14848], P(('groups', 'tokens')), parts along dimension 0, may hold values from -1000 to 1000
- keys_values: bfloat16 [4096, 1024], P(('groups', 'tokens')), parts along dimension 0, may hold values from -1000 to 1000
- plan: int32 [4096], P(('groups', 'tokens')), parts along dimension 0, may hold values from 0 to 2047, as said below
- doc_start: int32 [4096], P(('groups', 'tokens')), parts along dimension 0, may hold values from 0 to 2047, as said below
- keep_blocks: int32 [29, 2], replicated, may hold values from 0 to 3, all different within a row
- tile_owner: int32 [16], replicated, may hold values from 0 to 15, each once
Outputs:
- attended: bfloat16 [4096, 14848], P(('groups', 'tokens')), parts along dimension 0
- gram: float32 [32, 215296], P(('groups', 'tokens')), parts along dimension 0
The draws below stay inside these ranges and needn't reach their ends.
There are 2 independent parts, one for each index of `groups`. The reference program is written for one: setup_inputs(seed, part) draws one part's arguments, and reference() takes and returns one part's arrays. A program takes and returns all parts, laid end to end along the dimension named above; an argument that names none is the same for every part. Nothing has to cross between parts.
Inputs may be any that keep to these rules, and one draw needn't show every extreme that they name: `plan`: A permutation. Each device sends exactly 8 tokens to each device: the tokens of device s go to slots j of device d with (j % 128) // 8 == s. `doc_start`: never falls; documents lie whole inside aligned blocks of 128 slots, each block's first slot starts a document, and each block's last slot is a document of one token.
All inputs are finite; a program needn't handle non-finite values.
Results may differ from the reference program's by a relative error of at most 0.0027.
Values may be sent and summed in bfloat16 or wider, within the bound.
A program may use at most 128 MiB of HBM per device.

```python
import jax
import jax.numpy as jnp
from jax import lax

D = 14848
HEADS = 232
KV_HEADS = 8
HEAD_DIM = 64
BLOCK = 128
TOK_DEV = 128
TOKENS = 2048
SEND = 8
GROUPS = 29
KEPT = 7424
TW = 464
N_TOKENS = 16


def draw_queries(key, part):
    key = jax.random.fold_in(key, 1)
    base = jax.random.normal(jax.random.fold_in(key, 2), (TOKENS, D), jnp.float32)
    return base.astype(jnp.bfloat16)


def draw_keys_values(key, part):
    key = jax.random.fold_in(key, 7)
    width = KV_HEADS * HEAD_DIM
    base = jax.random.normal(jax.random.fold_in(key, 2), (TOKENS, 2 * width), jnp.float32)
    return base.astype(jnp.bfloat16)


def draw_plan(key, part):
    key = jax.random.fold_in(key, 11)
    sources = TOKENS // TOK_DEV
    place = jnp.arange(TOK_DEV, dtype=jnp.int32)
    anchor = jnp.arange(sources, dtype=jnp.int32)
    base = place[None, :] // SEND * TOK_DEV + anchor[:, None] * SEND + place[None, :] % SEND
    orders = jax.vmap(lambda k: jax.random.permutation(k, TOK_DEV))(jax.random.split(key, sources))
    return jnp.take_along_axis(base, orders.astype(jnp.int32), axis=1).reshape(TOKENS).astype(jnp.int32)


def draw_doc_start(key, part):
    key = jax.random.fold_in(key, 13)
    blocks = TOKENS // TOK_DEV
    rate = jax.random.randint(jax.random.fold_in(key, 1), (blocks, 1), 2, 80)
    roll = jax.random.randint(jax.random.fold_in(key, 2), (blocks, TOK_DEV), 0, 1000)
    place = jnp.arange(TOK_DEV, dtype=jnp.int32)[None, :]
    cut = (roll < rate) | (place == 0) | (place == TOK_DEV - 1)
    slots = jnp.arange(blocks, dtype=jnp.int32)[:, None] * TOK_DEV + place
    marks = jnp.where(cut, slots, 0)
    return lax.cummax(marks, axis=1).reshape(TOKENS).astype(jnp.int32)


def different_ones(stream_key, rows, number_of, top, lift):
    order = jax.random.permutation(jax.random.fold_in(stream_key, 1), number_of)
    pull = order
    for power in range(3):
        pull = pull * pull // number_of
    pull = pull * lift // number_of
    lots = jax.random.randint(jax.random.fold_in(stream_key, 2), (rows, number_of), 0, 4096) + pull
    holders = jax.random.permutation(jax.random.fold_in(stream_key, 3), rows)[jnp.arange(number_of) % rows]
    lots = jnp.where(jnp.arange(rows)[:, None] == holders[None, :], 1 << 14, lots)
    priority = lots * number_of + jnp.arange(number_of)
    return lax.top_k(priority.astype(jnp.int32), top)[1].astype(jnp.int32)


def setup_inputs(seed: int = 0, part: int = 0) -> dict:
    key_list = jax.random.split(jax.random.key(seed), 7)
    own_keys = jax.random.split(jax.random.fold_in(key_list[6], part), 7)
    return {
        "queries": draw_queries(jax.random.fold_in(jax.random.fold_in(key_list[6], part), 71), part),
        "keys_values": draw_keys_values(jax.random.fold_in(jax.random.fold_in(key_list[6], part), 71), part),
        "plan": draw_plan(jax.random.fold_in(jax.random.fold_in(key_list[6], part), 71), part),
        "doc_start": draw_doc_start(jax.random.fold_in(jax.random.fold_in(key_list[6], part), 71), part),
        "keep_blocks": different_ones(key_list[4], GROUPS, 4, 2, 0),
        "tile_owner": jax.random.permutation(key_list[5], N_TOKENS).astype(jnp.int32),
    }


def attend_block(q_block, kv_block, start_block):
    rows = q_block.shape[0]
    group = HEADS // KV_HEADS
    width = KV_HEADS * HEAD_DIM
    q4 = q_block.reshape(rows, KV_HEADS, group, HEAD_DIM).astype(jnp.float32)
    keys = kv_block[:, :width].reshape(rows, KV_HEADS, HEAD_DIM).astype(jnp.float32)
    values = kv_block[:, width:].reshape(rows, KV_HEADS, HEAD_DIM).astype(jnp.float32)
    scores = jnp.einsum('qkgd,skd->kgqs', q4, keys) / jnp.sqrt(jnp.float32(HEAD_DIM))
    place = jnp.arange(rows)
    allowed = (start_block[:, None] == start_block[None, :]) & (place[None, :] <= place[:, None])
    scores = jnp.where(allowed, scores, -jnp.inf)
    top = lax.optimization_barrier(jnp.max(scores, axis=-1, keepdims=True))
    weights = jnp.where(allowed, jnp.exp(scores - top), 0.0)
    totals = lax.optimization_barrier(jnp.sum(weights, axis=-1))
    rounded = weights.astype(jnp.bfloat16).astype(jnp.float32)
    mixed = jnp.einsum('kgqs,skd->qkgd', rounded, values)
    mixed = mixed / jnp.transpose(totals, (2, 0, 1))[..., None]
    return mixed.reshape(rows, -1).astype(jnp.bfloat16)

def compress(block, keep_blocks):
    rows = block.shape[0]
    split = block.reshape(rows, GROUPS, 4, BLOCK).astype(jnp.float32)
    picker = (keep_blocks[:, :, None] == jnp.arange(4, dtype=jnp.int32)[None, None, :]).astype(jnp.float32)
    kept = jnp.einsum('rgbc,gkb->rgkc', split, picker)
    return kept.reshape(rows, KEPT).astype(jnp.bfloat16)

def reference(queries, keys_values, plan, doc_start, keep_blocks, tile_owner):
    q_dest = jnp.zeros_like(queries).at[plan].set(queries)
    kv_dest = jnp.zeros_like(keys_values).at[plan].set(keys_values)
    blocks = (q_dest.reshape(N_TOKENS, TOK_DEV, D), kv_dest.reshape(N_TOKENS, TOK_DEV, -1), doc_start.reshape(N_TOKENS, TOK_DEV))
    out_dest = lax.map(lambda b: attend_block(b[0], b[1], b[2]), blocks).reshape(TOKENS, D)
    attended = out_dest[plan]
    kept = lax.map(lambda b: compress(b, keep_blocks), out_dest.reshape(N_TOKENS, TOK_DEV, D)).reshape(TOKENS, N_TOKENS, TW)

    def one_tile(tile):
        cols = lax.dynamic_index_in_dim(kept, tile, 1, keepdims=False)
        return jnp.dot(cols.T, cols, preferred_element_type=jnp.float32).reshape(TW * TW)
    gram = lax.map(one_tile, tile_owner) / jnp.float32(TOKENS)
    return (attended, gram)
```

```python
import functools

import jax
import jax.numpy as jnp
from jax import lax
from jax.experimental import pallas as pl
from jax.experimental.pallas import tpu as pltpu
from jax.sharding import PartitionSpec as P

HEADS = 232
KV_HEADS = 8
HEAD_DIM = 64
BLOCK = 128
GROUPS = 29
PAIRS = KV_HEADS // 2
SPAN = HEADS // KV_HEADS
HALF = SPAN // 2
PAD = 16


def attend_block(q_block, kv_block, start_block):
    rows = q_block.shape[0]
    group = HEADS // KV_HEADS
    width = KV_HEADS * HEAD_DIM
    q4 = q_block.reshape(rows, KV_HEADS, group, HEAD_DIM)
    keys = kv_block[:, :width].reshape(rows, KV_HEADS, HEAD_DIM)
    values = kv_block[:, width:].reshape(rows, KV_HEADS, HEAD_DIM)
    scores = jnp.einsum("qkgd,skd->kgqs", q4, keys, preferred_element_type=jnp.float32) / jnp.sqrt(
        jnp.float32(HEAD_DIM)
    )
    place = jnp.arange(rows)
    allowed = (start_block[:, None] == start_block[None, :]) & (place[None, :] <= place[:, None])
    scores = jnp.where(allowed, scores, -jnp.inf)
    top = jnp.max(scores, axis=-1, keepdims=True)
    weights = jnp.where(allowed, jnp.exp(scores - top), 0.0)
    totals = jnp.sum(weights, axis=-1)
    mixed = jnp.einsum(
        "kgqs,skd->qkgd", weights.astype(jnp.bfloat16), values, preferred_element_type=jnp.float32
    )
    mixed = mixed / jnp.transpose(totals, (2, 0, 1))[..., None]
    return mixed.reshape(rows, -1).astype(jnp.bfloat16)


def compress(block, keep_blocks):
    rows = block.shape[0]
    split = block.reshape(rows, GROUPS, 4, BLOCK)
    picker = (keep_blocks[:, :, None] == jnp.arange(4, dtype=jnp.int32)[None, None, :]).astype(
        jnp.bfloat16
    )
    kept = jnp.einsum("rgbc,gkb->rgkc", split, picker, preferred_element_type=jnp.float32)
    return kept.reshape(rows, -1).astype(jnp.bfloat16)


def general(queries, keys_values, plan, doc_start, keep_blocks, tile_owner):
    rows = queries.shape[0]
    devices = lax.axis_size("tokens")
    send = rows // devices
    target = plan // rows
    place = target * send + plan % rows % send
    order = jnp.zeros((rows,), jnp.int32).at[place].set(jnp.arange(rows, dtype=jnp.int32))
    q_dest, kv_dest = (
        lax.all_to_all(queries[order], "tokens", split_axis=0, concat_axis=0, tiled=True),
        lax.all_to_all(keys_values[order], "tokens", split_axis=0, concat_axis=0, tiled=True),
    )
    out_dest = attend_block(q_dest, kv_dest, doc_start)
    returned = lax.all_to_all(out_dest, "tokens", split_axis=0, concat_axis=0, tiled=True)
    attended = returned[place]
    kept = compress(out_dest, keep_blocks)
    tiles = jnp.transpose(kept.reshape(rows, devices, -1), (1, 0, 2))[tile_owner]
    mine = lax.all_to_all(tiles, "tokens", split_axis=0, concat_axis=0, tiled=True)
    mine = mine.reshape(rows * devices, -1)
    square = jnp.einsum("ra,rb->ab", mine, mine, preferred_element_type=jnp.float32)
    return (attended, square.reshape(1, -1) / jnp.float32(rows * devices))


def attention_kernel(
    devices, tw, keep_ref, owner_ref, place_ref, q_ref, k_ref, v_ref, st_ref, out_ref, send_ref,
    q3, kf, vf, o3, oall, inv,
):
    p = pl.program_id(0)
    me = lax.axis_index("tokens")
    rows = q_ref.shape[0]
    send = rows // devices
    f32, bf16 = jnp.float32, jnp.bfloat16
    spot = lax.broadcasted_iota(jnp.int32, (rows, rows), 0)
    pick = (place_ref[...] == spot).astype(f32)
    back = pick.T.astype(bf16)
    pick = pick.astype(bf16)
    for t in range(SPAN):
        tile = jnp.dot(pick, q_ref[:, t * 128 : (t + 1) * 128], preferred_element_type=f32)
        q3[t] = tile * 0.125
    kf[...] = k_ref[...].astype(f32)
    vf[...] = v_ref[...].astype(f32)

    low = lax.broadcasted_iota(jnp.int32, (rows, 128), 1) < 64
    row8 = lax.broadcasted_iota(jnp.int32, (send, rows), 0) + me * send
    col8 = lax.broadcasted_iota(jnp.int32, (send, rows), 1)

    def two(tile):
        turned = pltpu.roll(tile, 64, 1)
        first = jnp.concatenate([jnp.where(low, tile, 0.0), jnp.where(low, 0.0, turned)], 0)
        second = jnp.concatenate([jnp.where(low, turned, 0.0), jnp.where(low, 0.0, tile)], 0)
        return first.astype(bf16), second.astype(bf16)

    cut = HALF * send

    def block(d, carry):
        at = pl.ds(pl.multiple_of(d * send, send), send)
        ka, kb = two(kf[:, at, :].reshape(rows, 128))
        va, vb = two(vf[:, at, :].reshape(rows, 128))
        starts = jnp.broadcast_to(st_ref[d, 0:1, :].astype(f32), (send, rows))
        start = jnp.sum(jnp.where(col8 == row8, starts, 0.0), axis=1, keepdims=True)
        allowed = ((col8.astype(f32) >= start) & (col8 <= row8))[None]
        qa = q3[0 : HALF + 1, at, :].reshape(cut + send, 128).astype(bf16)
        qb = q3[HALF:SPAN, at, :].reshape(cut + send, 128).astype(bf16)
        nt = (((1,), (1,)), ((), ()))
        sa = lax.dot_general(qa, ka, nt, preferred_element_type=f32)
        sb = lax.dot_general(qb, kb, nt, preferred_element_type=f32)

        def soft(s):
            s = s.reshape(-1, send, rows)
            s = jnp.where(allowed, s, -jnp.inf)
            top = jnp.max(s, axis=-1, keepdims=True)
            w = jnp.exp(s - top)
            total = jnp.sum(w, axis=-1, keepdims=True)
            return w.reshape(-1, rows), total.reshape(-1, 1)

        left = jnp.concatenate([sa[:, :rows], sb[send:, :rows]], 0)
        right = jnp.concatenate([sa[:cut, rows:], sb[:, rows:]], 0)
        wl, tl = soft(left)
        wr, tr = soft(right)
        zero = jnp.zeros((send, rows), f32)
        wa = jnp.concatenate(
            [wl[: cut + send], jnp.concatenate([wr[:cut], zero], 0)], 1
        ).astype(bf16)
        wb = jnp.concatenate(
            [jnp.concatenate([zero, wl[cut + send :]], 0), wr[cut:]], 1
        ).astype(bf16)
        oa = jnp.dot(wa, va, preferred_element_type=f32)
        ob = jnp.dot(wb, vb, preferred_element_type=f32)
        mixed = jnp.concatenate([oa[:cut], oa[cut:] + ob[:send], ob[send:]], 0)
        lane = lax.broadcasted_iota(jnp.int32, mixed.shape, 1) < 64
        mixed = mixed / jnp.where(lane, tl, tr)
        o3[:, at, :] = mixed.reshape(SPAN, send, 128)
        return carry

    lax.fori_loop(0, devices, block, 0)

    for t in range(SPAN):
        tile = o3[t].astype(bf16)
        out_ref[:, t * 128 : (t + 1) * 128] = jnp.dot(
            back, tile, preferred_element_type=f32
        ).astype(bf16)
        oall[p * SPAN + t] = tile

    @pl.when(p == PAIRS - 1)
    def _():
        for d in range(devices):
            inv[owner_ref[d]] = d
        width = send_ref.shape[2]
        lane = lax.broadcasted_iota(jnp.int32, (rows, 128), 1)
        for t in range(devices):
            first, shift = divmod(t * tw, 128)
            blocks = []
            for b in range(first, (t * tw + tw - 1) // 128 + 1):
                tile = oall[4 * (b // 2) + keep_ref[b // 2, b % 2]].astype(f32)
                blocks.append(pltpu.roll(tile, 128 - shift, 1) if shift else tile)
            for j in range(width // 128):
                piece = blocks[j]
                if shift and j + 1 < len(blocks):
                    piece = jnp.where(lane < 128 - shift, piece, blocks[j + 1])
                left = tw - j * 128
                if left < 128:
                    piece = jnp.where(lane < left, piece, 0.0)
                send_ref[inv[t], :, j * 128 : (j + 1) * 128] = piece.astype(bf16)


def flatten_into(square, flat_ref, tw):
    rows = tw // 8
    step = tw * 8 // 128
    pieces = square.shape[0]
    lane = lax.broadcasted_iota(jnp.int32, (rows, 128), 1)
    total = [None] * step
    for a in range(8):
        first, shift = divmod(a * tw, 128)
        parts = [square[j, pl.ds(a, rows, stride=8), :] for j in range(pieces)]
        if shift:
            parts = [pltpu.roll(x, shift, 1) for x in parts]
        for j in range(pieces + 1):
            if first + j >= step:
                continue
            if not shift:
                if j == pieces:
                    continue
                part = parts[j]
            elif j == 0:
                part = jnp.where(lane >= shift, parts[0], 0.0)
            elif j == pieces:
                part = jnp.where(lane < shift, parts[-1], 0.0)
            else:
                part = jnp.where(lane >= shift, parts[j], parts[j - 1])
            old = total[first + j]
            total[first + j] = part if old is None else old + part
    for i in range(step):
        flat_ref[pl.ds(i, rows, stride=step), :] = total[i]


def gram_kernel(tw, scale, x_ref, flat_ref, square):
    x = x_ref[...]
    full = lax.dot_general(x, x, (((0,), (0,)), ((), ())), preferred_element_type=jnp.float32)
    for j in range(square.shape[0]):
        square[j] = full[:tw, j * 128 : (j + 1) * 128] * scale
    flatten_into(square, flat_ref, tw)


def blocked(queries, keys_values, plan, doc_start, keep_blocks, tile_owner):
    rows, width = queries.shape
    devices = lax.axis_size("tokens")
    send = rows // devices
    tw = GROUPS * 2 * BLOCK // devices
    wide = -(-tw // 128) * 128
    span = SPAN * 128
    place = plan // rows * send + plan % send
    pick = (place[None, :] == jnp.arange(rows, dtype=jnp.int32)[:, None]).astype(jnp.bfloat16)
    kv_sorted = jnp.dot(pick, keys_values, preferred_element_type=jnp.float32).astype(jnp.bfloat16)
    starts = (doc_start % rows).astype(jnp.bfloat16)
    extra = jnp.pad(starts[None, :], ((0, PAD - 1), (0, keys_values.shape[1] - rows)))
    gathered = lax.all_gather(jnp.concatenate([kv_sorted, extra], 0), "tokens")
    vmem = functools.partial(pl.BlockSpec, memory_space=pltpu.VMEM)
    attended, tiles = pl.pallas_call(
        functools.partial(attention_kernel, devices, tw),
        grid=(PAIRS,),
        in_specs=[
            pl.BlockSpec(memory_space=pltpu.SMEM),
            pl.BlockSpec(memory_space=pltpu.SMEM),
            vmem((1, rows), lambda p: (0, 0)),
            vmem((rows, span), lambda p: (0, p)),
            vmem((devices, rows, 128), lambda p: (0, 0, p)),
            vmem((devices, rows, 128), lambda p: (0, 0, PAIRS + p)),
            vmem((devices, PAD, 128), lambda p: (0, rows // PAD, 0)),
        ],
        out_specs=[
            vmem((rows, span), lambda p: (0, p)),
            vmem((devices, rows, wide), lambda p: (0, 0, 0)),
        ],
        out_shape=[
            jax.ShapeDtypeStruct((rows, width), jnp.bfloat16),
            jax.ShapeDtypeStruct((devices, rows, wide), jnp.bfloat16),
        ],
        scratch_shapes=[
            pltpu.VMEM((SPAN, rows, 128), jnp.float32),
            pltpu.VMEM((devices, rows, 128), jnp.float32),
            pltpu.VMEM((devices, rows, 128), jnp.float32),
            pltpu.VMEM((SPAN, rows, 128), jnp.float32),
            pltpu.VMEM((PAIRS * SPAN, rows, 128), jnp.bfloat16),
            pltpu.SMEM((devices,), jnp.int32),
        ],
        compiler_params=pltpu.CompilerParams(vmem_limit_bytes=50 * 1024 * 1024),
    )(keep_blocks, tile_owner, place[None, :], queries, gathered, gathered, gathered)
    mine = lax.all_to_all(tiles, "tokens", split_axis=0, concat_axis=0, tiled=True)
    mine = mine.reshape(rows * devices, wide)
    flat = pl.pallas_call(
        functools.partial(gram_kernel, tw, 1.0 / (rows * devices)),
        out_shape=jax.ShapeDtypeStruct((tw * tw // 128, 128), jnp.float32),
        scratch_shapes=[pltpu.VMEM((wide // 128, tw, 128), jnp.float32)],
        compiler_params=pltpu.CompilerParams(vmem_limit_bytes=40 * 1024 * 1024),
    )(mine)
    return attended, flat.reshape(1, tw * tw)


def solution(mesh):
    in_specs = (
        P(("groups", "tokens"), None),
        P(("groups", "tokens"), None),
        P(("groups", "tokens")),
        P(("groups", "tokens")),
        P(),
        P(),
    )
    out_specs = (P(("groups", "tokens"), None), P(("groups", "tokens"), None))
    local = blocked if mesh.shape["tokens"] == 16 else general
    return jax.shard_map(local, mesh=mesh, in_specs=in_specs, out_specs=out_specs, check_vma=False)
```

```python
import functools

import jax
import jax.numpy as jnp
from jax import lax
from jax.experimental import pallas as pl
from jax.experimental.pallas import tpu as pltpu
from jax.sharding import PartitionSpec as P

HEADS = 232
KV_HEADS = 8
HEAD_DIM = 64
BLOCK = 128
GROUPS = 29
PAIRS = KV_HEADS // 2
SPAN = HEADS // KV_HEADS
HALF = SPAN // 2
PAD = 16


def attend_block(q_block, kv_block, start_block):
    rows = q_block.shape[0]
    group = HEADS // KV_HEADS
    width = KV_HEADS * HEAD_DIM
    q4 = q_block.reshape(rows, KV_HEADS, group, HEAD_DIM)
    keys = kv_block[:, :width].reshape(rows, KV_HEADS, HEAD_DIM)
    values = kv_block[:, width:].reshape(rows, KV_HEADS, HEAD_DIM)
    scores = jnp.einsum("qkgd,skd->kgqs", q4, keys, preferred_element_type=jnp.float32) / jnp.sqrt(
        jnp.float32(HEAD_DIM)
    )
    place = jnp.arange(rows)
    allowed = (start_block[:, None] == start_block[None, :]) & (place[None, :] <= place[:, None])
    scores = jnp.where(allowed, scores, -jnp.inf)
    top = jnp.max(scores, axis=-1, keepdims=True)
    weights = jnp.where(allowed, jnp.exp(scores - top), 0.0)
    totals = jnp.sum(weights, axis=-1)
    mixed = jnp.einsum(
        "kgqs,skd->qkgd", weights.astype(jnp.bfloat16), values, preferred_element_type=jnp.float32
    )
    mixed = mixed / jnp.transpose(totals, (2, 0, 1))[..., None]
    return mixed.reshape(rows, -1).astype(jnp.bfloat16)


def compress(block, keep_blocks):
    rows = block.shape[0]
    split = block.reshape(rows, GROUPS, 4, BLOCK)
    picker = (keep_blocks[:, :, None] == jnp.arange(4, dtype=jnp.int32)[None, None, :]).astype(
        jnp.bfloat16
    )
    kept = jnp.einsum("rgbc,gkb->rgkc", split, picker, preferred_element_type=jnp.float32)
    return kept.reshape(rows, -1).astype(jnp.bfloat16)


def general(queries, keys_values, plan, doc_start, keep_blocks, tile_owner):
    rows = queries.shape[0]
    devices = lax.axis_size("tokens")
    send = rows // devices
    target = plan // rows
    place = target * send + plan % rows % send
    order = jnp.zeros((rows,), jnp.int32).at[place].set(jnp.arange(rows, dtype=jnp.int32))
    q_dest, kv_dest = (
        lax.all_to_all(queries[order], "tokens", split_axis=0, concat_axis=0, tiled=True),
        lax.all_to_all(keys_values[order], "tokens", split_axis=0, concat_axis=0, tiled=True),
    )
    out_dest = attend_block(q_dest, kv_dest, doc_start)
    returned = lax.all_to_all(out_dest, "tokens", split_axis=0, concat_axis=0, tiled=True)
    attended = returned[place]
    kept = compress(out_dest, keep_blocks)
    tiles = jnp.transpose(kept.reshape(rows, devices, -1), (1, 0, 2))[tile_owner]
    mine = lax.all_to_all(tiles, "tokens", split_axis=0, concat_axis=0, tiled=True)
    mine = mine.reshape(rows * devices, -1)
    square = jnp.einsum("ra,rb->ab", mine, mine, preferred_element_type=jnp.float32)
    return (attended, square.reshape(1, -1) / jnp.float32(rows * devices))


def gather_kernel(zs, ys, mine_ref, all_ref, own_sem, recv, sent):
    me = lax.axis_index("tokens")
    z, y, c = me // (2 * ys), me // 2 % ys, me % 2
    side = (z * ys + (1 - y)) * 2 + c
    core = (z * ys + y) * 2 + 1 - c
    up, down = z < zs - 1, z > 0

    def index(zz, yy, cc):
        return (zz * ys + yy) * 2 + cc

    def push(slot, kind, to):
        copy = pltpu.make_async_remote_copy(
            src_ref=all_ref.at[slot],
            dst_ref=all_ref.at[slot],
            send_sem=sent.at[kind, slot],
            recv_sem=recv.at[slot],
            device_id={"tokens": to},
            device_id_type=pl.DeviceIdType.MESH,
        )
        return copy

    barrier = pltpu.get_barrier_semaphore()

    def greet(to):
        pl.semaphore_signal(
            barrier, inc=1, device_id={"tokens": to}, device_id_type=pl.DeviceIdType.MESH
        )

    greet(side)
    greet(core)
    pl.when(up)(lambda: greet(me + 2 * ys))
    pl.when(down)(lambda: greet(me - 2 * ys))
    pl.semaphore_wait(barrier, 2 + up.astype(jnp.int32) + down.astype(jnp.int32))

    local = pltpu.make_async_copy(mine_ref, all_ref.at[me], own_sem)
    local.start()
    local.wait()

    def step(k, finish):
        for sign in (1, -1) if k else (0,):
            source = z - sign * k
            inside = (source >= 0) & (source < zs)
            slot = index(jnp.clip(source, 0, zs - 1), y, c)

            def do():
                def act(copy):
                    copy.wait_send() if finish else copy.start()

                if k and not finish:
                    push(slot, 0, core).wait_recv()
                if sign >= 0:
                    pl.when(up)(lambda: act(push(slot, 0, me + 2 * ys)))
                if sign <= 0:
                    pl.when(down)(lambda: act(push(slot, 1, me - 2 * ys)))
                act(push(slot, 2, side))
                act(push(slot, 3, core))

            pl.when(inside)(do)
        for sign in (1, -1) if k else (0,):
            source = z - sign * k
            inside = (source >= 0) & (source < zs)
            slot = index(jnp.clip(source, 0, zs - 1), 1 - y, c)

            def across():
                copy = push(slot, 3, core)
                if finish:
                    copy.wait_send()
                else:
                    copy.wait_recv()
                    copy.start()

            pl.when(inside)(across)

    for k in range(zs):
        step(k, False)
    for zz in range(zs):
        for yy in range(ys):
            push(index(zz, yy, 1 - c), 3, core).wait_recv()
    for k in range(zs):
        step(k, True)


def gather(block, devices):
    ys = 2
    zs = devices // (2 * ys)
    return pl.pallas_call(
        functools.partial(gather_kernel, zs, ys),
        out_shape=jax.ShapeDtypeStruct((devices,) + block.shape, block.dtype),
        in_specs=[pl.BlockSpec(memory_space=pl.ANY)],
        out_specs=pl.BlockSpec(memory_space=pl.ANY),
        scratch_shapes=[
            pltpu.SemaphoreType.DMA,
            pltpu.SemaphoreType.DMA((devices,)),
            pltpu.SemaphoreType.DMA((4, devices)),
        ],
        compiler_params=pltpu.CompilerParams(collective_id=0, has_side_effects=True),
    )(block)


def attention_kernel(
    devices, tw, keep_ref, owner_ref, place_ref, q_ref, k_ref, v_ref, st_ref, out_ref, send_ref,
    q3, kf, vf, o3, oall, inv,
):
    p = pl.program_id(0)
    me = lax.axis_index("tokens")
    rows = q_ref.shape[0]
    send = rows // devices
    f32, bf16 = jnp.float32, jnp.bfloat16
    spot = lax.broadcasted_iota(jnp.int32, (rows, rows), 0)
    pick = (place_ref[...] == spot).astype(f32)
    back = pick.T.astype(bf16)
    pick = pick.astype(bf16)
    for t in range(SPAN):
        tile = jnp.dot(pick, q_ref[:, t * 128 : (t + 1) * 128], preferred_element_type=f32)
        q3[t] = tile * 0.125
    kf[...] = k_ref[...].astype(f32)
    vf[...] = v_ref[...].astype(f32)

    low = lax.broadcasted_iota(jnp.int32, (rows, 128), 1) < 64
    row8 = lax.broadcasted_iota(jnp.int32, (send, rows), 0) + me * send
    col8 = lax.broadcasted_iota(jnp.int32, (send, rows), 1)

    def two(tile):
        turned = pltpu.roll(tile, 64, 1)
        first = jnp.concatenate([jnp.where(low, tile, 0.0), jnp.where(low, 0.0, turned)], 0)
        second = jnp.concatenate([jnp.where(low, turned, 0.0), jnp.where(low, 0.0, tile)], 0)
        return first.astype(bf16), second.astype(bf16)

    cut = HALF * send

    def block(d, carry):
        at = pl.ds(pl.multiple_of(d * send, send), send)
        ka, kb = two(kf[:, at, :].reshape(rows, 128))
        va, vb = two(vf[:, at, :].reshape(rows, 128))
        starts = jnp.broadcast_to(st_ref[d, 0:1, :].astype(f32), (send, rows))
        start = jnp.sum(jnp.where(col8 == row8, starts, 0.0), axis=1, keepdims=True)
        allowed = ((col8.astype(f32) >= start) & (col8 <= row8))[None]
        qa = q3[0 : HALF + 1, at, :].reshape(cut + send, 128).astype(bf16)
        qb = q3[HALF:SPAN, at, :].reshape(cut + send, 128).astype(bf16)
        nt = (((1,), (1,)), ((), ()))
        sa = lax.dot_general(qa, ka, nt, preferred_element_type=f32)
        sb = lax.dot_general(qb, kb, nt, preferred_element_type=f32)

        def soft(s):
            s = s.reshape(-1, send, rows)
            s = jnp.where(allowed, s, -jnp.inf)
            top = jnp.max(s, axis=-1, keepdims=True)
            w = jnp.exp(s - top)
            total = jnp.sum(w, axis=-1, keepdims=True)
            return w.reshape(-1, rows), total.reshape(-1, 1)

        left = jnp.concatenate([sa[:, :rows], sb[send:, :rows]], 0)
        right = jnp.concatenate([sa[:cut, rows:], sb[:, rows:]], 0)
        wl, tl = soft(left)
        wr, tr = soft(right)
        zero = jnp.zeros((send, rows), f32)
        wa = jnp.concatenate(
            [wl[: cut + send], jnp.concatenate([wr[:cut], zero], 0)], 1
        ).astype(bf16)
        wb = jnp.concatenate(
            [jnp.concatenate([zero, wl[cut + send :]], 0), wr[cut:]], 1
        ).astype(bf16)
        oa = jnp.dot(wa, va, preferred_element_type=f32)
        ob = jnp.dot(wb, vb, preferred_element_type=f32)
        mixed = jnp.concatenate([oa[:cut], oa[cut:] + ob[:send], ob[send:]], 0)
        lane = lax.broadcasted_iota(jnp.int32, mixed.shape, 1) < 64
        mixed = mixed / jnp.where(lane, tl, tr)
        o3[:, at, :] = mixed.reshape(SPAN, send, 128)
        return carry

    lax.fori_loop(0, devices, block, 0)

    for t in range(SPAN):
        tile = o3[t].astype(bf16)
        out_ref[:, t * 128 : (t + 1) * 128] = jnp.dot(
            back, tile, preferred_element_type=f32
        ).astype(bf16)
        oall[p * SPAN + t] = tile

    @pl.when(p == PAIRS - 1)
    def _():
        for d in range(devices):
            inv[owner_ref[d]] = d
        for b in range(2 * GROUPS):
            tile = oall[4 * (b // 2) + keep_ref[b // 2, b % 2]].astype(f32).T.astype(bf16)
            for t in range(b * 128 // tw, (b * 128 + 127) // tw + 1):
                first, last = max(b * 128, t * tw), min(b * 128 + 128, t * tw + tw)
                send_ref[inv[t], first - t * tw : last - t * tw, :] = tile[
                    first - b * 128 : last - b * 128
                ]


def flatten_into(square, flat_ref, tw):
    rows = tw // 8
    step = tw * 8 // 128
    pieces = square.shape[0]
    lane = lax.broadcasted_iota(jnp.int32, (rows, 128), 1)
    total = [None] * step
    for a in range(8):
        first, shift = divmod(a * tw, 128)
        parts = [square[j, pl.ds(a, rows, stride=8), :] for j in range(pieces)]
        if shift:
            parts = [pltpu.roll(x, shift, 1) for x in parts]
        for j in range(pieces + 1):
            if first + j >= step:
                continue
            if not shift:
                if j == pieces:
                    continue
                part = parts[j]
            elif j == 0:
                part = jnp.where(lane >= shift, parts[0], 0.0)
            elif j == pieces:
                part = jnp.where(lane < shift, parts[-1], 0.0)
            else:
                part = jnp.where(lane >= shift, parts[j], parts[j - 1])
            old = total[first + j]
            total[first + j] = part if old is None else old + part
    for i in range(step):
        flat_ref[pl.ds(i, rows, stride=step), :] = total[i]


def gram_kernel(tw, scale, x_ref, flat_ref, square, rowwise):
    x = jnp.concatenate([x_ref[s] for s in range(x_ref.shape[0])], 1)
    width = square.shape[0] * 128
    other = jnp.concatenate([x, jnp.zeros((width - tw, x.shape[1]), x.dtype)], 0)
    full = lax.dot_general(x, other, (((1,), (1,)), ((), ())), preferred_element_type=jnp.float32)
    for j in range(square.shape[0]):
        square[j] = full[:, j * 128 : (j + 1) * 128] * scale
    flatten_into(square, rowwise, tw)
    lines = rowwise.shape[0]
    for i in range(0, lines, 8):
        n = min(8, lines - i)
        flat_ref[0:1, i * 128 : (i + n) * 128] = rowwise[i : i + n, :].reshape(1, n * 128)


def blocked(queries, keys_values, plan, doc_start, keep_blocks, tile_owner):
    rows, width = queries.shape
    devices = lax.axis_size("tokens")
    send = rows // devices
    tw = GROUPS * 2 * BLOCK // devices
    wide = -(-tw // 128) * 128
    span = SPAN * 128
    place = plan // rows * send + plan % send
    pick = (place[None, :] == jnp.arange(rows, dtype=jnp.int32)[:, None]).astype(jnp.bfloat16)
    kv_sorted = jnp.dot(pick, keys_values, preferred_element_type=jnp.float32).astype(jnp.bfloat16)
    starts = (doc_start % rows).astype(jnp.bfloat16)
    extra = jnp.pad(starts[None, :], ((0, PAD - 1), (0, keys_values.shape[1] - rows)))
    gathered = gather(jnp.concatenate([kv_sorted, extra], 0), devices)
    vmem = functools.partial(pl.BlockSpec, memory_space=pltpu.VMEM)
    attended, tiles = pl.pallas_call(
        functools.partial(attention_kernel, devices, tw),
        grid=(PAIRS,),
        in_specs=[
            pl.BlockSpec(memory_space=pltpu.SMEM),
            pl.BlockSpec(memory_space=pltpu.SMEM),
            vmem((1, rows), lambda p: (0, 0)),
            vmem((rows, span), lambda p: (0, p)),
            vmem((devices, rows, 128), lambda p: (0, 0, p)),
            vmem((devices, rows, 128), lambda p: (0, 0, PAIRS + p)),
            vmem((devices, PAD, 128), lambda p: (0, rows // PAD, 0)),
        ],
        out_specs=[
            vmem((rows, span), lambda p: (0, p)),
            vmem((devices, tw, rows), lambda p: (0, 0, 0)),
        ],
        out_shape=[
            jax.ShapeDtypeStruct((rows, width), jnp.bfloat16),
            jax.ShapeDtypeStruct((devices, tw, rows), jnp.bfloat16),
        ],
        scratch_shapes=[
            pltpu.VMEM((SPAN, rows, 128), jnp.float32),
            pltpu.VMEM((devices, rows, 128), jnp.float32),
            pltpu.VMEM((devices, rows, 128), jnp.float32),
            pltpu.VMEM((SPAN, rows, 128), jnp.float32),
            pltpu.VMEM((PAIRS * SPAN, rows, 128), jnp.bfloat16),
            pltpu.SMEM((devices,), jnp.int32),
        ],
        compiler_params=pltpu.CompilerParams(vmem_limit_bytes=50 * 1024 * 1024),
    )(keep_blocks, tile_owner, place[None, :], queries, gathered, gathered, gathered)
    mine = lax.all_to_all(tiles, "tokens", split_axis=0, concat_axis=0, tiled=True)
    flat = pl.pallas_call(
        functools.partial(gram_kernel, tw, 1.0 / (rows * devices)),
        out_shape=jax.ShapeDtypeStruct((1, tw * tw), jnp.float32),
        scratch_shapes=[
            pltpu.VMEM((wide // 128, tw, 128), jnp.float32),
            pltpu.VMEM((tw * tw // 128, 128), jnp.float32),
        ],
        compiler_params=pltpu.CompilerParams(vmem_limit_bytes=40 * 1024 * 1024),
    )(mine)
    return attended, flat


def solution(mesh):
    in_specs = (
        P(("groups", "tokens"), None),
        P(("groups", "tokens"), None),
        P(("groups", "tokens")),
        P(("groups", "tokens")),
        P(),
        P(),
    )
    out_specs = (P(("groups", "tokens"), None), P(("groups", "tokens"), None))
    local = blocked if mesh.shape["tokens"] == 16 else general
    return jax.shard_map(local, mesh=mesh, in_specs=in_specs, out_specs=out_specs, check_vma=False)
```

```python
import functools

import jax
import jax.numpy as jnp
from jax import lax
from jax.experimental import pallas as pl
from jax.experimental.pallas import tpu as pltpu
from jax.sharding import PartitionSpec as P

HEADS = 232
KV_HEADS = 8
HEAD_DIM = 64
BLOCK = 128
GROUPS = 29
PAIRS = KV_HEADS // 2
SPAN = HEADS // KV_HEADS
HALF = SPAN // 2
PAD = 16


def attend_block(q_block, kv_block, start_block):
    rows = q_block.shape[0]
    group = HEADS // KV_HEADS
    width = KV_HEADS * HEAD_DIM
    q4 = q_block.reshape(rows, KV_HEADS, group, HEAD_DIM)
    keys = kv_block[:, :width].reshape(rows, KV_HEADS, HEAD_DIM)
    values = kv_block[:, width:].reshape(rows, KV_HEADS, HEAD_DIM)
    scores = jnp.einsum("qkgd,skd->kgqs", q4, keys, preferred_element_type=jnp.float32) / jnp.sqrt(
        jnp.float32(HEAD_DIM)
    )
    place = jnp.arange(rows)
    allowed = (start_block[:, None] == start_block[None, :]) & (place[None, :] <= place[:, None])
    scores = jnp.where(allowed, scores, -jnp.inf)
    top = jnp.max(scores, axis=-1, keepdims=True)
    weights = jnp.where(allowed, jnp.exp(scores - top), 0.0)
    totals = jnp.sum(weights, axis=-1)
    mixed = jnp.einsum(
        "kgqs,skd->qkgd", weights.astype(jnp.bfloat16), values, preferred_element_type=jnp.float32
    )
    mixed = mixed / jnp.transpose(totals, (2, 0, 1))[..., None]
    return mixed.reshape(rows, -1).astype(jnp.bfloat16)


def compress(block, keep_blocks):
    rows = block.shape[0]
    split = block.reshape(rows, GROUPS, 4, BLOCK)
    picker = (keep_blocks[:, :, None] == jnp.arange(4, dtype=jnp.int32)[None, None, :]).astype(
        jnp.bfloat16
    )
    kept = jnp.einsum("rgbc,gkb->rgkc", split, picker, preferred_element_type=jnp.float32)
    return kept.reshape(rows, -1).astype(jnp.bfloat16)


def general(queries, keys_values, plan, doc_start, keep_blocks, tile_owner):
    rows = queries.shape[0]
    devices = lax.axis_size("tokens")
    send = rows // devices
    target = plan // rows
    place = target * send + plan % rows % send
    order = jnp.zeros((rows,), jnp.int32).at[place].set(jnp.arange(rows, dtype=jnp.int32))
    q_dest, kv_dest = (
        lax.all_to_all(queries[order], "tokens", split_axis=0, concat_axis=0, tiled=True),
        lax.all_to_all(keys_values[order], "tokens", split_axis=0, concat_axis=0, tiled=True),
    )
    out_dest = attend_block(q_dest, kv_dest, doc_start)
    returned = lax.all_to_all(out_dest, "tokens", split_axis=0, concat_axis=0, tiled=True)
    attended = returned[place]
    kept = compress(out_dest, keep_blocks)
    tiles = jnp.transpose(kept.reshape(rows, devices, -1), (1, 0, 2))[tile_owner]
    mine = lax.all_to_all(tiles, "tokens", split_axis=0, concat_axis=0, tiled=True)
    mine = mine.reshape(rows * devices, -1)
    square = jnp.einsum("ra,rb->ab", mine, mine, preferred_element_type=jnp.float32)
    return (attended, square.reshape(1, -1) / jnp.float32(rows * devices))


def attention_kernel(
    devices, place_ref, q_ref, k_ref, v_ref, st_ref, *rest
):
    out_ref, tiles_ref, q3, kf, vf, o3 = rest[-6:]
    me = lax.axis_index("tokens")
    rows = q_ref.shape[0]
    send = rows // devices
    f32, bf16 = jnp.float32, jnp.bfloat16
    spot = lax.broadcasted_iota(jnp.int32, (rows, rows), 0)
    pick = (place_ref[...] == spot).astype(f32)
    back = pick.T.astype(bf16)
    pick = pick.astype(bf16)
    for t in range(SPAN):
        tile = jnp.dot(pick, q_ref[:, t * 128 : (t + 1) * 128], preferred_element_type=f32)
        q3[t] = tile * 0.125
    kf[...] = k_ref[...].astype(f32)
    vf[...] = v_ref[...].astype(f32)

    low = lax.broadcasted_iota(jnp.int32, (rows, 128), 1) < 64
    row8 = lax.broadcasted_iota(jnp.int32, (send, rows), 0) + me * send
    col8 = lax.broadcasted_iota(jnp.int32, (send, rows), 1)

    def two(tile):
        turned = pltpu.roll(tile, 64, 1)
        first = jnp.concatenate([jnp.where(low, tile, 0.0), jnp.where(low, 0.0, turned)], 0)
        second = jnp.concatenate([jnp.where(low, turned, 0.0), jnp.where(low, 0.0, tile)], 0)
        return first.astype(bf16), second.astype(bf16)

    cut = HALF * send

    def block(d, carry):
        at = pl.ds(pl.multiple_of(d * send, send), send)
        ka, kb = two(kf[:, at, :].reshape(rows, 128))
        va, vb = two(vf[:, at, :].reshape(rows, 128))
        starts = jnp.broadcast_to(st_ref[d, 0:1, :].astype(f32), (send, rows))
        start = jnp.sum(jnp.where(col8 == row8, starts, 0.0), axis=1, keepdims=True)
        allowed = ((col8.astype(f32) >= start) & (col8 <= row8))[None]
        qa = q3[0 : HALF + 1, at, :].reshape(cut + send, 128).astype(bf16)
        qb = q3[HALF:SPAN, at, :].reshape(cut + send, 128).astype(bf16)
        nt = (((1,), (1,)), ((), ()))
        sa = lax.dot_general(qa, ka, nt, preferred_element_type=f32)
        sb = lax.dot_general(qb, kb, nt, preferred_element_type=f32)

        def soft(s):
            s = s.reshape(-1, send, rows)
            s = jnp.where(allowed, s, -jnp.inf)
            top = jnp.max(s, axis=-1, keepdims=True)
            w = jnp.exp(s - top)
            total = jnp.sum(w, axis=-1, keepdims=True)
            return w.reshape(-1, rows), total.reshape(-1, 1)

        left = jnp.concatenate([sa[:, :rows], sb[send:, :rows]], 0)
        right = jnp.concatenate([sa[:cut, rows:], sb[:, rows:]], 0)
        wl, tl = soft(left)
        wr, tr = soft(right)
        zero = jnp.zeros((send, rows), f32)
        wa = jnp.concatenate(
            [wl[: cut + send], jnp.concatenate([wr[:cut], zero], 0)], 1
        ).astype(bf16)
        wb = jnp.concatenate(
            [jnp.concatenate([zero, wl[cut + send :]], 0), wr[cut:]], 1
        ).astype(bf16)
        oa = jnp.dot(wa, va, preferred_element_type=f32)
        ob = jnp.dot(wb, vb, preferred_element_type=f32)
        mixed = jnp.concatenate([oa[:cut], oa[cut:] + ob[:send], ob[send:]], 0)
        lane = lax.broadcasted_iota(jnp.int32, mixed.shape, 1) < 64
        mixed = mixed / jnp.where(lane, tl, tr)
        o3[:, at, :] = mixed.reshape(SPAN, send, 128)
        return carry

    lax.fori_loop(0, devices, block, 0)

    for t in range(SPAN):
        tile = o3[t].astype(bf16)
        out_ref[:, t * 128 : (t + 1) * 128] = jnp.dot(
            back, tile, preferred_element_type=f32
        ).astype(bf16)
        tiles_ref[t] = tile


def pack_kernel(devices, tw, keep_ref, owner_ref, *rest):
    parts, send_ref, oall, inv = rest[:PAIRS], rest[-3], rest[-2], rest[-1]
    for p in range(PAIRS):
        oall[p * SPAN : (p + 1) * SPAN] = parts[p][...]
    for d in range(devices):
        inv[owner_ref[d]] = d
    for b in range(2 * GROUPS):
        tile = oall[4 * (b // 2) + keep_ref[b // 2, b % 2]].astype(jnp.float32).T.astype(jnp.bfloat16)
        for t in range(b * 128 // tw, (b * 128 + 127) // tw + 1):
            first, last = max(b * 128, t * tw), min(b * 128 + 128, t * tw + tw)
            send_ref[inv[t], first - t * tw : last - t * tw, :] = tile[
                first - b * 128 : last - b * 128
            ]


def flatten_into(square, flat_ref, tw):
    rows = tw // 8
    step = tw * 8 // 128
    pieces = square.shape[0]
    lane = lax.broadcasted_iota(jnp.int32, (rows, 128), 1)
    total = [None] * step
    for a in range(8):
        first, shift = divmod(a * tw, 128)
        parts = [square[j, pl.ds(a, rows, stride=8), :] for j in range(pieces)]
        if shift:
            parts = [pltpu.roll(x, shift, 1) for x in parts]
        for j in range(pieces + 1):
            if first + j >= step:
                continue
            if not shift:
                if j == pieces:
                    continue
                part = parts[j]
            elif j == 0:
                part = jnp.where(lane >= shift, parts[0], 0.0)
            elif j == pieces:
                part = jnp.where(lane < shift, parts[-1], 0.0)
            else:
                part = jnp.where(lane >= shift, parts[j], parts[j - 1])
            old = total[first + j]
            total[first + j] = part if old is None else old + part
    for i in range(step):
        flat_ref[pl.ds(i, rows, stride=step), :] = total[i]


def gram_kernel(tw, scale, x_ref, flat_ref, square, rowwise):
    x = jnp.concatenate([x_ref[s] for s in range(x_ref.shape[0])], 1)
    width = square.shape[0] * 128
    other = jnp.concatenate([x, jnp.zeros((width - tw, x.shape[1]), x.dtype)], 0)
    full = lax.dot_general(x, other, (((1,), (1,)), ((), ())), preferred_element_type=jnp.float32)
    for j in range(square.shape[0]):
        square[j] = full[:, j * 128 : (j + 1) * 128] * scale
    flatten_into(square, rowwise, tw)
    lines = rowwise.shape[0]
    for i in range(0, lines, 8):
        n = min(8, lines - i)
        flat_ref[0:1, i * 128 : (i + n) * 128] = rowwise[i : i + n, :].reshape(1, n * 128)


def blocked(queries, keys_values, plan, doc_start, keep_blocks, tile_owner):
    rows, width = queries.shape
    devices = lax.axis_size("tokens")
    send = rows // devices
    tw = GROUPS * 2 * BLOCK // devices
    wide = -(-tw // 128) * 128
    span = SPAN * 128
    place = plan // rows * send + plan % send
    pick = (place[None, :] == jnp.arange(rows, dtype=jnp.int32)[:, None]).astype(jnp.bfloat16)
    kv_sorted = jnp.dot(pick, keys_values, preferred_element_type=jnp.float32).astype(jnp.bfloat16)
    starts = (doc_start % rows).astype(jnp.bfloat16)
    extra = jnp.pad(starts[None, :], ((0, PAD - 1), (0, 256 - rows)))
    half = KV_HEADS * HEAD_DIM
    vmem = functools.partial(pl.BlockSpec, memory_space=pltpu.VMEM)
    parts, gathered, attended = [], [], None

    def send_pair(p):
        load = jnp.concatenate(
            [kv_sorted[:, p * 128 : p * 128 + 128], kv_sorted[:, half + p * 128 : half + p * 128 + 128]],
            1,
        )
        if p == 0:
            load = jnp.concatenate([load, extra], 0)
        else:
            load, gathered[-1] = lax.optimization_barrier((load, gathered[-1]))
        if p >= 2:
            load, parts[p - 2] = lax.optimization_barrier((load, parts[p - 2]))
        gathered.append(lax.all_gather(load, "tokens"))

    send_pair(0)
    for p in range(PAIRS):
        if p + 1 < PAIRS:
            send_pair(p + 1)
        more = [] if attended is None else [attended]
        attended, part = pl.pallas_call(
            functools.partial(attention_kernel, devices),
            grid=(1,),
            in_specs=[
                vmem((1, rows), lambda i: (0, 0)),
                vmem((rows, span), lambda i, p=p: (0, p)),
                vmem((devices, rows, 128), lambda i: (0, 0, 0)),
                vmem((devices, rows, 128), lambda i: (0, 0, 1)),
                vmem((devices, PAD, 128), lambda i: (0, rows // PAD, 0)),
            ]
            + [pl.BlockSpec(memory_space=pl.ANY)] * len(more),
            out_specs=[
                vmem((rows, span), lambda i, p=p: (0, p)),
                vmem((SPAN, rows, 128), lambda i: (0, 0, 0)),
            ],
            out_shape=[
                jax.ShapeDtypeStruct((rows, width), jnp.bfloat16),
                jax.ShapeDtypeStruct((SPAN, rows, 128), jnp.bfloat16),
            ],
            scratch_shapes=[
                pltpu.VMEM((SPAN, rows, 128), jnp.float32),
                pltpu.VMEM((devices, rows, 128), jnp.float32),
                pltpu.VMEM((devices, rows, 128), jnp.float32),
                pltpu.VMEM((SPAN, rows, 128), jnp.float32),
            ],
            input_output_aliases={5: 0} if more else {},
            cost_estimate=pl.CostEstimate(
                flops=10_000_000_000, bytes_accessed=4_000_000, transcendentals=1_000_000
            ),
            compiler_params=pltpu.CompilerParams(vmem_limit_bytes=50 * 1024 * 1024),
        )(place[None, :], queries, gathered[p], gathered[p], gathered[0], *more)
        parts.append(part)
    tiles = pl.pallas_call(
        functools.partial(pack_kernel, devices, tw),
        in_specs=[pl.BlockSpec(memory_space=pltpu.SMEM)] * 2
        + [pl.BlockSpec(memory_space=pltpu.VMEM)] * PAIRS,
        out_specs=pl.BlockSpec(memory_space=pltpu.VMEM),
        out_shape=jax.ShapeDtypeStruct((devices, tw, rows), jnp.bfloat16),
        scratch_shapes=[
            pltpu.VMEM((PAIRS * SPAN, rows, 128), jnp.bfloat16),
            pltpu.SMEM((devices,), jnp.int32),
        ],
        compiler_params=pltpu.CompilerParams(vmem_limit_bytes=50 * 1024 * 1024),
    )(keep_blocks, tile_owner, *parts)
    mine = lax.all_to_all(tiles, "tokens", split_axis=0, concat_axis=0, tiled=True)
    flat = pl.pallas_call(
        functools.partial(gram_kernel, tw, 1.0 / (rows * devices)),
        out_shape=jax.ShapeDtypeStruct((1, tw * tw), jnp.float32),
        scratch_shapes=[
            pltpu.VMEM((wide // 128, tw, 128), jnp.float32),
            pltpu.VMEM((tw * tw // 128, 128), jnp.float32),
        ],
        compiler_params=pltpu.CompilerParams(vmem_limit_bytes=40 * 1024 * 1024),
    )(mine)
    return attended, flat


def solution(mesh):
    in_specs = (
        P(("groups", "tokens"), None),
        P(("groups", "tokens"), None),
        P(("groups", "tokens")),
        P(("groups", "tokens")),
        P(),
        P(),
    )
    out_specs = (P(("groups", "tokens"), None), P(("groups", "tokens"), None))
    local = blocked if mesh.shape["tokens"] == 16 else general
    return jax.shard_map(local, mesh=mesh, in_specs=in_specs, out_specs=out_specs, check_vma=False)
```

```python
import functools

import jax
import jax.numpy as jnp
from jax import lax
from jax.experimental import pallas as pl
from jax.experimental.pallas import tpu as pltpu
from jax.sharding import PartitionSpec as P

HEADS = 232
KV_HEADS = 8
HEAD_DIM = 64
BLOCK = 128
GROUPS = 29
PAIRS = KV_HEADS // 2
SPAN = HEADS // KV_HEADS
HALF = SPAN // 2
PAD = 16


def attend_block(q_block, kv_block, start_block):
    rows = q_block.shape[0]
    group = HEADS // KV_HEADS
    width = KV_HEADS * HEAD_DIM
    q4 = q_block.reshape(rows, KV_HEADS, group, HEAD_DIM)
    keys = kv_block[:, :width].reshape(rows, KV_HEADS, HEAD_DIM)
    values = kv_block[:, width:].reshape(rows, KV_HEADS, HEAD_DIM)
    scores = jnp.einsum("qkgd,skd->kgqs", q4, keys, preferred_element_type=jnp.float32) / jnp.sqrt(
        jnp.float32(HEAD_DIM)
    )
    place = jnp.arange(rows)
    allowed = (start_block[:, None] == start_block[None, :]) & (place[None, :] <= place[:, None])
    scores = jnp.where(allowed, scores, -jnp.inf)
    top = jnp.max(scores, axis=-1, keepdims=True)
    weights = jnp.where(allowed, jnp.exp(scores - top), 0.0)
    totals = jnp.sum(weights, axis=-1)
    mixed = jnp.einsum(
        "kgqs,skd->qkgd", weights.astype(jnp.bfloat16), values, preferred_element_type=jnp.float32
    )
    mixed = mixed / jnp.transpose(totals, (2, 0, 1))[..., None]
    return mixed.reshape(rows, -1).astype(jnp.bfloat16)


def compress(block, keep_blocks):
    rows = block.shape[0]
    split = block.reshape(rows, GROUPS, 4, BLOCK)
    picker = (keep_blocks[:, :, None] == jnp.arange(4, dtype=jnp.int32)[None, None, :]).astype(
        jnp.bfloat16
    )
    kept = jnp.einsum("rgbc,gkb->rgkc", split, picker, preferred_element_type=jnp.float32)
    return kept.reshape(rows, -1).astype(jnp.bfloat16)


def general(queries, keys_values, plan, doc_start, keep_blocks, tile_owner):
    rows = queries.shape[0]
    devices = lax.axis_size("tokens")
    send = rows // devices
    target = plan // rows
    place = target * send + plan % rows % send
    order = jnp.zeros((rows,), jnp.int32).at[place].set(jnp.arange(rows, dtype=jnp.int32))
    q_dest, kv_dest = (
        lax.all_to_all(queries[order], "tokens", split_axis=0, concat_axis=0, tiled=True),
        lax.all_to_all(keys_values[order], "tokens", split_axis=0, concat_axis=0, tiled=True),
    )
    out_dest = attend_block(q_dest, kv_dest, doc_start)
    returned = lax.all_to_all(out_dest, "tokens", split_axis=0, concat_axis=0, tiled=True)
    attended = returned[place]
    kept = compress(out_dest, keep_blocks)
    tiles = jnp.transpose(kept.reshape(rows, devices, -1), (1, 0, 2))[tile_owner]
    mine = lax.all_to_all(tiles, "tokens", split_axis=0, concat_axis=0, tiled=True)
    mine = mine.reshape(rows * devices, -1)
    square = jnp.einsum("ra,rb->ab", mine, mine, preferred_element_type=jnp.float32)
    return (attended, square.reshape(1, -1) / jnp.float32(rows * devices))


def gather_kernel(zs, ys, mine_ref, all_ref, own_sem, recv, sent):
    me = lax.axis_index("tokens")
    z, y, c = me // (2 * ys), me // 2 % ys, me % 2
    side = (z * ys + (1 - y)) * 2 + c
    core = (z * ys + y) * 2 + 1 - c
    up, down = z < zs - 1, z > 0

    def index(zz, yy, cc):
        return (zz * ys + yy) * 2 + cc

    def push(slot, kind, to):
        copy = pltpu.make_async_remote_copy(
            src_ref=all_ref.at[slot],
            dst_ref=all_ref.at[slot],
            send_sem=sent.at[kind, slot],
            recv_sem=recv.at[slot],
            device_id={"tokens": to},
            device_id_type=pl.DeviceIdType.MESH,
        )
        return copy

    barrier = pltpu.get_barrier_semaphore()

    def greet(to):
        pl.semaphore_signal(
            barrier, inc=1, device_id={"tokens": to}, device_id_type=pl.DeviceIdType.MESH
        )

    greet(side)
    greet(core)
    pl.when(up)(lambda: greet(me + 2 * ys))
    pl.when(down)(lambda: greet(me - 2 * ys))
    pl.semaphore_wait(barrier, 2 + up.astype(jnp.int32) + down.astype(jnp.int32))

    local = pltpu.make_async_copy(mine_ref, all_ref.at[me], own_sem)
    local.start()
    local.wait()

    def step(k, finish):
        for sign in (1, -1) if k else (0,):
            source = z - sign * k
            inside = (source >= 0) & (source < zs)
            slot = index(jnp.clip(source, 0, zs - 1), y, c)

            def do():
                def act(copy):
                    copy.wait_send() if finish else copy.start()

                if k and not finish:
                    push(slot, 0, core).wait_recv()
                if sign >= 0:
                    pl.when(up)(lambda: act(push(slot, 0, me + 2 * ys)))
                if sign <= 0:
                    pl.when(down)(lambda: act(push(slot, 1, me - 2 * ys)))
                act(push(slot, 2, side))
                act(push(slot, 3, core))

            pl.when(inside)(do)
        for sign in (1, -1) if k else (0,):
            source = z - sign * k
            inside = (source >= 0) & (source < zs)
            slot = index(jnp.clip(source, 0, zs - 1), 1 - y, c)

            def across():
                copy = push(slot, 3, core)
                if finish:
                    copy.wait_send()
                else:
                    copy.wait_recv()
                    copy.start()

            pl.when(inside)(across)

    for k in range(zs):
        step(k, False)
    for zz in range(zs):
        for yy in range(ys):
            push(index(zz, yy, 1 - c), 3, core).wait_recv()
    for k in range(zs):
        step(k, True)


def gather(block, devices):
    ys = 2
    zs = devices // (2 * ys)
    return pl.pallas_call(
        functools.partial(gather_kernel, zs, ys),
        out_shape=jax.ShapeDtypeStruct((devices,) + block.shape, block.dtype),
        in_specs=[pl.BlockSpec(memory_space=pltpu.VMEM)],
        out_specs=pl.BlockSpec(memory_space=pltpu.VMEM),
        scratch_shapes=[
            pltpu.SemaphoreType.DMA,
            pltpu.SemaphoreType.DMA((devices,)),
            pltpu.SemaphoreType.DMA((4, devices)),
        ],
        compiler_params=pltpu.CompilerParams(
            collective_id=0, has_side_effects=True, vmem_limit_bytes=20 * 1024 * 1024
        ),
    )(block)


def attention_kernel(
    devices, tw, keep_ref, owner_ref, place_ref, q_ref, k_ref, v_ref, st_ref, out_ref, send_ref,
    q3, kf, vf, o3, oall, inv,
):
    p = pl.program_id(0)
    me = lax.axis_index("tokens")
    rows = q_ref.shape[0]
    send = rows // devices
    f32, bf16 = jnp.float32, jnp.bfloat16
    spot = lax.broadcasted_iota(jnp.int32, (rows, rows), 0)
    pick = (place_ref[...] == spot).astype(f32)
    back = pick.T.astype(bf16)
    pick = pick.astype(bf16)
    for t in range(SPAN):
        tile = jnp.dot(pick, q_ref[:, t * 128 : (t + 1) * 128], preferred_element_type=f32)
        q3[t] = tile * 0.125
    kf[...] = k_ref[...].astype(f32)
    vf[...] = v_ref[...].astype(f32)

    low = lax.broadcasted_iota(jnp.int32, (rows, 128), 1) < 64
    row8 = lax.broadcasted_iota(jnp.int32, (send, rows), 0) + me * send
    col8 = lax.broadcasted_iota(jnp.int32, (send, rows), 1)

    def two(tile):
        turned = pltpu.roll(tile, 64, 1)
        first = jnp.concatenate([jnp.where(low, tile, 0.0), jnp.where(low, 0.0, turned)], 0)
        second = jnp.concatenate([jnp.where(low, turned, 0.0), jnp.where(low, 0.0, tile)], 0)
        return first.astype(bf16), second.astype(bf16)

    cut = HALF * send

    def block(d, carry):
        at = pl.ds(pl.multiple_of(d * send, send), send)
        ka, kb = two(kf[:, at, :].reshape(rows, 128))
        va, vb = two(vf[:, at, :].reshape(rows, 128))
        starts = jnp.broadcast_to(st_ref[d, 0:1, :].astype(f32), (send, rows))
        start = jnp.sum(jnp.where(col8 == row8, starts, 0.0), axis=1, keepdims=True)
        allowed = ((col8.astype(f32) >= start) & (col8 <= row8))[None]
        qa = q3[0 : HALF + 1, at, :].reshape(cut + send, 128).astype(bf16)
        qb = q3[HALF:SPAN, at, :].reshape(cut + send, 128).astype(bf16)
        nt = (((1,), (1,)), ((), ()))
        sa = lax.dot_general(qa, ka, nt, preferred_element_type=f32)
        sb = lax.dot_general(qb, kb, nt, preferred_element_type=f32)

        def soft(s):
            s = s.reshape(-1, send, rows)
            s = jnp.where(allowed, s, -jnp.inf)
            top = jnp.max(s, axis=-1, keepdims=True)
            w = jnp.exp(s - top)
            total = jnp.sum(w, axis=-1, keepdims=True)
            return w.reshape(-1, rows), total.reshape(-1, 1)

        left = jnp.concatenate([sa[:, :rows], sb[send:, :rows]], 0)
        right = jnp.concatenate([sa[:cut, rows:], sb[:, rows:]], 0)
        wl, tl = soft(left)
        wr, tr = soft(right)
        zero = jnp.zeros((send, rows), f32)
        wa = jnp.concatenate(
            [wl[: cut + send], jnp.concatenate([wr[:cut], zero], 0)], 1
        ).astype(bf16)
        wb = jnp.concatenate(
            [jnp.concatenate([zero, wl[cut + send :]], 0), wr[cut:]], 1
        ).astype(bf16)
        oa = jnp.dot(wa, va, preferred_element_type=f32)
        ob = jnp.dot(wb, vb, preferred_element_type=f32)
        mixed = jnp.concatenate([oa[:cut], oa[cut:] + ob[:send], ob[send:]], 0)
        lane = lax.broadcasted_iota(jnp.int32, mixed.shape, 1) < 64
        mixed = mixed / jnp.where(lane, tl, tr)
        o3[:, at, :] = mixed.reshape(SPAN, send, 128)
        return carry

    lax.fori_loop(0, devices, block, 0, unroll=2)

    for t in range(SPAN):
        tile = o3[t].astype(bf16)
        out_ref[:, t * 128 : (t + 1) * 128] = jnp.dot(
            back, tile, preferred_element_type=f32
        ).astype(bf16)
        oall[p * SPAN + t] = tile

    @pl.when(p == PAIRS - 1)
    def _():
        for d in range(devices):
            inv[owner_ref[d]] = d
        for b in range(2 * GROUPS):
            tile = oall[4 * (b // 2) + keep_ref[b // 2, b % 2]].astype(f32).T.astype(bf16)
            for t in range(b * 128 // tw, (b * 128 + 127) // tw + 1):
                first, last = max(b * 128, t * tw), min(b * 128 + 128, t * tw + tw)
                send_ref[inv[t], first - t * tw : last - t * tw, :] = tile[
                    first - b * 128 : last - b * 128
                ]


def flatten_into(square, flat_ref, tw):
    rows = tw // 8
    step = tw * 8 // 128
    pieces = square.shape[0]
    lane = lax.broadcasted_iota(jnp.int32, (rows, 128), 1)
    total = [None] * step
    for a in range(8):
        first, shift = divmod(a * tw, 128)
        parts = [square[j, pl.ds(a, rows, stride=8), :] for j in range(pieces)]
        if shift:
            parts = [pltpu.roll(x, shift, 1) for x in parts]
        for j in range(pieces + 1):
            if first + j >= step:
                continue
            if not shift:
                if j == pieces:
                    continue
                part = parts[j]
            elif j == 0:
                part = jnp.where(lane >= shift, parts[0], 0.0)
            elif j == pieces:
                part = jnp.where(lane < shift, parts[-1], 0.0)
            else:
                part = jnp.where(lane >= shift, parts[j], parts[j - 1])
            old = total[first + j]
            total[first + j] = part if old is None else old + part
    for i in range(step):
        flat_ref[pl.ds(i, rows, stride=step), :] = total[i]


def gram_kernel(tw, scale, x_ref, flat_ref, square, rowwise):
    x = jnp.concatenate([x_ref[s] for s in range(x_ref.shape[0])], 1)
    width = square.shape[0] * 128
    other = jnp.concatenate([x, jnp.zeros((width - tw, x.shape[1]), x.dtype)], 0)
    full = lax.dot_general(x, other, (((1,), (1,)), ((), ())), preferred_element_type=jnp.float32)
    for j in range(square.shape[0]):
        square[j] = full[:, j * 128 : (j + 1) * 128] * scale
    flatten_into(square, rowwise, tw)
    lines = rowwise.shape[0]
    for i in range(0, lines, 8):
        n = min(8, lines - i)
        flat_ref[0:1, i * 128 : (i + n) * 128] = rowwise[i : i + n, :].reshape(1, n * 128)


def blocked(queries, keys_values, plan, doc_start, keep_blocks, tile_owner):
    rows, width = queries.shape
    devices = lax.axis_size("tokens")
    send = rows // devices
    tw = GROUPS * 2 * BLOCK // devices
    wide = -(-tw // 128) * 128
    span = SPAN * 128
    place = plan // rows * send + plan % send
    pick = (place[None, :] == jnp.arange(rows, dtype=jnp.int32)[:, None]).astype(jnp.bfloat16)
    kv_sorted = jnp.dot(pick, keys_values, preferred_element_type=jnp.float32).astype(jnp.bfloat16)
    starts = (doc_start % rows).astype(jnp.bfloat16)
    extra = jnp.pad(starts[None, :], ((0, PAD - 1), (0, keys_values.shape[1] - rows)))
    gathered = gather(jnp.concatenate([kv_sorted, extra], 0), devices)
    vmem = functools.partial(pl.BlockSpec, memory_space=pltpu.VMEM)
    attended, tiles = pl.pallas_call(
        functools.partial(attention_kernel, devices, tw),
        grid=(PAIRS,),
        in_specs=[
            pl.BlockSpec(memory_space=pltpu.SMEM),
            pl.BlockSpec(memory_space=pltpu.SMEM),
            vmem((1, rows), lambda p: (0, 0)),
            vmem((rows, span), lambda p: (0, p)),
            vmem((devices, rows, 128), lambda p: (0, 0, p)),
            vmem((devices, rows, 128), lambda p: (0, 0, PAIRS + p)),
            vmem((devices, PAD, 128), lambda p: (0, rows // PAD, 0)),
        ],
        out_specs=[
            vmem((rows, span), lambda p: (0, p)),
            vmem((devices, tw, rows), lambda p: (0, 0, 0)),
        ],
        out_shape=[
            jax.ShapeDtypeStruct((rows, width), jnp.bfloat16),
            jax.ShapeDtypeStruct((devices, tw, rows), jnp.bfloat16),
        ],
        scratch_shapes=[
            pltpu.VMEM((SPAN, rows, 128), jnp.float32),
            pltpu.VMEM((devices, rows, 128), jnp.float32),
            pltpu.VMEM((devices, rows, 128), jnp.float32),
            pltpu.VMEM((SPAN, rows, 128), jnp.float32),
            pltpu.VMEM((PAIRS * SPAN, rows, 128), jnp.bfloat16),
            pltpu.SMEM((devices,), jnp.int32),
        ],
        compiler_params=pltpu.CompilerParams(vmem_limit_bytes=50 * 1024 * 1024),
    )(keep_blocks, tile_owner, place[None, :], queries, gathered, gathered, gathered)
    mine = lax.all_to_all(tiles, "tokens", split_axis=0, concat_axis=0, tiled=True)
    flat = pl.pallas_call(
        functools.partial(gram_kernel, tw, 1.0 / (rows * devices)),
        out_shape=jax.ShapeDtypeStruct((1, tw * tw), jnp.float32),
        scratch_shapes=[
            pltpu.VMEM((wide // 128, tw, 128), jnp.float32),
            pltpu.VMEM((tw * tw // 128, 128), jnp.float32),
        ],
        compiler_params=pltpu.CompilerParams(vmem_limit_bytes=40 * 1024 * 1024),
    )(mine)
    return attended, flat


def solution(mesh):
    in_specs = (
        P(("groups", "tokens"), None),
        P(("groups", "tokens"), None),
        P(("groups", "tokens")),
        P(("groups", "tokens")),
        P(),
        P(),
    )
    out_specs = (P(("groups", "tokens"), None), P(("groups", "tokens"), None))
    local = blocked if mesh.shape["tokens"] == 16 else general
    return jax.shard_map(local, mesh=mesh, in_specs=in_specs, out_specs=out_specs, check_vma=False)
```

```python
import functools

import jax
import jax.numpy as jnp
from jax import lax
from jax.experimental import pallas as pl
from jax.experimental.pallas import tpu as pltpu
from jax.sharding import PartitionSpec as P

HEADS = 232
KV_HEADS = 8
HEAD_DIM = 64
BLOCK = 128
GROUPS = 29
PAIRS = KV_HEADS // 2
SPAN = HEADS // KV_HEADS
HALF = SPAN // 2
PAD = 16


def attend_block(q_block, kv_block, start_block):
    rows = q_block.shape[0]
    group = HEADS // KV_HEADS
    width = KV_HEADS * HEAD_DIM
    q4 = q_block.reshape(rows, KV_HEADS, group, HEAD_DIM)
    keys = kv_block[:, :width].reshape(rows, KV_HEADS, HEAD_DIM)
    values = kv_block[:, width:].reshape(rows, KV_HEADS, HEAD_DIM)
    scores = jnp.einsum("qkgd,skd->kgqs", q4, keys, preferred_element_type=jnp.float32) / jnp.sqrt(
        jnp.float32(HEAD_DIM)
    )
    place = jnp.arange(rows)
    allowed = (start_block[:, None] == start_block[None, :]) & (place[None, :] <= place[:, None])
    scores = jnp.where(allowed, scores, -jnp.inf)
    top = jnp.max(scores, axis=-1, keepdims=True)
    weights = jnp.where(allowed, jnp.exp(scores - top), 0.0)
    totals = jnp.sum(weights, axis=-1)
    mixed = jnp.einsum(
        "kgqs,skd->qkgd", weights.astype(jnp.bfloat16), values, preferred_element_type=jnp.float32
    )
    mixed = mixed / jnp.transpose(totals, (2, 0, 1))[..., None]
    return mixed.reshape(rows, -1).astype(jnp.bfloat16)


def compress(block, keep_blocks):
    rows = block.shape[0]
    split = block.reshape(rows, GROUPS, 4, BLOCK)
    picker = (keep_blocks[:, :, None] == jnp.arange(4, dtype=jnp.int32)[None, None, :]).astype(
        jnp.bfloat16
    )
    kept = jnp.einsum("rgbc,gkb->rgkc", split, picker, preferred_element_type=jnp.float32)
    return kept.reshape(rows, -1).astype(jnp.bfloat16)


def general(queries, keys_values, plan, doc_start, keep_blocks, tile_owner):
    rows = queries.shape[0]
    devices = lax.axis_size("tokens")
    send = rows // devices
    target = plan // rows
    place = target * send + plan % rows % send
    order = jnp.zeros((rows,), jnp.int32).at[place].set(jnp.arange(rows, dtype=jnp.int32))
    q_dest, kv_dest = (
        lax.all_to_all(queries[order], "tokens", split_axis=0, concat_axis=0, tiled=True),
        lax.all_to_all(keys_values[order], "tokens", split_axis=0, concat_axis=0, tiled=True),
    )
    out_dest = attend_block(q_dest, kv_dest, doc_start)
    returned = lax.all_to_all(out_dest, "tokens", split_axis=0, concat_axis=0, tiled=True)
    attended = returned[place]
    kept = compress(out_dest, keep_blocks)
    tiles = jnp.transpose(kept.reshape(rows, devices, -1), (1, 0, 2))[tile_owner]
    mine = lax.all_to_all(tiles, "tokens", split_axis=0, concat_axis=0, tiled=True)
    mine = mine.reshape(rows * devices, -1)
    square = jnp.einsum("ra,rb->ab", mine, mine, preferred_element_type=jnp.float32)
    return (attended, square.reshape(1, -1) / jnp.float32(rows * devices))


def gather_kernel(zs, ys, mine_ref, all_ref, own_sem, recv, sent):
    me = lax.axis_index("tokens")
    z, y, c = me // (2 * ys), me // 2 % ys, me % 2
    side = (z * ys + (1 - y)) * 2 + c
    core = (z * ys + y) * 2 + 1 - c
    up, down = z < zs - 1, z > 0

    def index(zz, yy, cc):
        return (zz * ys + yy) * 2 + cc

    def push(slot, kind, to):
        copy = pltpu.make_async_remote_copy(
            src_ref=all_ref.at[slot],
            dst_ref=all_ref.at[slot],
            send_sem=sent.at[kind, slot],
            recv_sem=recv.at[slot],
            device_id={"tokens": to},
            device_id_type=pl.DeviceIdType.MESH,
        )
        return copy

    barrier = pltpu.get_barrier_semaphore()

    def greet(to):
        pl.semaphore_signal(
            barrier, inc=1, device_id={"tokens": to}, device_id_type=pl.DeviceIdType.MESH
        )

    greet(side)
    greet(core)
    pl.when(up)(lambda: greet(me + 2 * ys))
    pl.when(down)(lambda: greet(me - 2 * ys))
    pl.semaphore_wait(barrier, 2 + up.astype(jnp.int32) + down.astype(jnp.int32))

    local = pltpu.make_async_copy(mine_ref, all_ref.at[me], own_sem)
    local.start()
    local.wait()

    def step(k, finish):
        for sign in (1, -1) if k else (0,):
            source = z - sign * k
            inside = (source >= 0) & (source < zs)
            slot = index(jnp.clip(source, 0, zs - 1), y, c)

            def do():
                def act(copy):
                    copy.wait_send() if finish else copy.start()

                if k and not finish:
                    push(slot, 0, core).wait_recv()
                if sign >= 0:
                    pl.when(up)(lambda: act(push(slot, 0, me + 2 * ys)))
                if sign <= 0:
                    pl.when(down)(lambda: act(push(slot, 1, me - 2 * ys)))
                act(push(slot, 2, side))
                act(push(slot, 3, core))

            pl.when(inside)(do)
        for sign in (1, -1) if k else (0,):
            source = z - sign * k
            inside = (source >= 0) & (source < zs)
            slot = index(jnp.clip(source, 0, zs - 1), 1 - y, c)

            def across():
                copy = push(slot, 3, core)
                if finish:
                    copy.wait_send()
                else:
                    copy.wait_recv()
                    copy.start()

            pl.when(inside)(across)

    for k in range(zs):
        step(k, False)
    for zz in range(zs):
        for yy in range(ys):
            push(index(zz, yy, 1 - c), 3, core).wait_recv()
    for k in range(zs):
        step(k, True)


def gather(block, devices):
    ys = 2
    zs = devices // (2 * ys)
    return pl.pallas_call(
        functools.partial(gather_kernel, zs, ys),
        out_shape=jax.ShapeDtypeStruct((devices,) + block.shape, block.dtype),
        in_specs=[pl.BlockSpec(memory_space=pltpu.VMEM)],
        out_specs=pl.BlockSpec(memory_space=pltpu.VMEM),
        scratch_shapes=[
            pltpu.SemaphoreType.DMA,
            pltpu.SemaphoreType.DMA((devices,)),
            pltpu.SemaphoreType.DMA((4, devices)),
        ],
        compiler_params=pltpu.CompilerParams(
            collective_id=0, has_side_effects=True, vmem_limit_bytes=20 * 1024 * 1024
        ),
    )(block)


def attention_kernel(
    devices, tw, keep_ref, owner_ref, place_ref, q_ref, k_ref, v_ref, st_ref, out_ref, send_ref,
    q3, kf, vf, o3, oall, inv,
):
    p = pl.program_id(0)
    me = lax.axis_index("tokens")
    rows = q_ref.shape[0]
    send = rows // devices
    f32, bf16 = jnp.float32, jnp.bfloat16
    spot = lax.broadcasted_iota(jnp.int32, (rows, rows), 0)
    pick = (place_ref[...] == spot).astype(f32)
    back = pick.T.astype(bf16)
    pick = pick.astype(bf16)
    for t in range(SPAN):
        tile = jnp.dot(pick, q_ref[:, t * 128 : (t + 1) * 128], preferred_element_type=f32)
        q3[t] = tile * 0.125
    kf[...] = k_ref[...].astype(f32)
    vf[...] = v_ref[...].astype(f32)

    low = lax.broadcasted_iota(jnp.int32, (rows, 128), 1) < 64
    row8 = lax.broadcasted_iota(jnp.int32, (send, rows), 0) + me * send
    col8 = lax.broadcasted_iota(jnp.int32, (send, rows), 1)

    def two(tile):
        turned = pltpu.roll(tile, 64, 1)
        first = jnp.concatenate([jnp.where(low, tile, 0.0), jnp.where(low, 0.0, turned)], 0)
        second = jnp.concatenate([jnp.where(low, turned, 0.0), jnp.where(low, 0.0, tile)], 0)
        return first.astype(bf16), second.astype(bf16)

    cut = HALF * send

    def block(d, carry):
        at = pl.ds(pl.multiple_of(d * send, send), send)
        ka, kb = two(kf[:, at, :].reshape(rows, 128))
        va, vb = two(vf[:, at, :].reshape(rows, 128))
        starts = jnp.broadcast_to(st_ref[d, 0:1, :].astype(f32), (send, rows))
        start = jnp.sum(jnp.where(col8 == row8, starts, 0.0), axis=1, keepdims=True)
        allowed = ((col8.astype(f32) >= start) & (col8 <= row8))[None]
        qa = q3[0 : HALF + 1, at, :].reshape(cut + send, 128).astype(bf16)
        qb = q3[HALF:SPAN, at, :].reshape(cut + send, 128).astype(bf16)
        nt = (((1,), (1,)), ((), ()))
        sa = lax.dot_general(qa, ka, nt, preferred_element_type=f32)
        sb = lax.dot_general(qb, kb, nt, preferred_element_type=f32)

        def soft(s):
            s = s.reshape(-1, send, rows)
            s = jnp.where(allowed, s, -jnp.inf)
            top = jnp.max(s, axis=-1, keepdims=True)
            w = jnp.exp(s - top)
            total = jnp.sum(w, axis=-1, keepdims=True)
            return w.reshape(-1, rows), total.reshape(-1, 1)

        left = jnp.concatenate([sa[:, :rows], sb[send:, :rows]], 0)
        right = jnp.concatenate([sa[:cut, rows:], sb[:, rows:]], 0)
        wl, tl = soft(left)
        wr, tr = soft(right)
        zero = jnp.zeros((send, rows), f32)
        wa = jnp.concatenate(
            [wl[: cut + send], jnp.concatenate([wr[:cut], zero], 0)], 1
        ).astype(bf16)
        wb = jnp.concatenate(
            [jnp.concatenate([zero, wl[cut + send :]], 0), wr[cut:]], 1
        ).astype(bf16)
        oa = jnp.dot(wa, va, preferred_element_type=f32)
        ob = jnp.dot(wb, vb, preferred_element_type=f32)
        mixed = jnp.concatenate([oa[:cut], oa[cut:] + ob[:send], ob[send:]], 0)
        lane = lax.broadcasted_iota(jnp.int32, mixed.shape, 1) < 64
        mixed = mixed / jnp.where(lane, tl, tr)
        o3[:, at, :] = mixed.reshape(SPAN, send, 128)
        return carry

    lax.fori_loop(0, devices, block, 0, unroll=4)

    for t in range(SPAN):
        tile = o3[t].astype(bf16)
        out_ref[:, t * 128 : (t + 1) * 128] = jnp.dot(
            back, tile, preferred_element_type=f32
        ).astype(bf16)
        oall[p * SPAN + t] = tile

    @pl.when(p == PAIRS - 1)
    def _():
        for d in range(devices):
            inv[owner_ref[d]] = d
        for b in range(2 * GROUPS):
            tile = oall[4 * (b // 2) + keep_ref[b // 2, b % 2]].astype(f32).T.astype(bf16)
            for t in range(b * 128 // tw, (b * 128 + 127) // tw + 1):
                first, last = max(b * 128, t * tw), min(b * 128 + 128, t * tw + tw)
                send_ref[inv[t], first - t * tw : last - t * tw, :] = tile[
                    first - b * 128 : last - b * 128
                ]


def flatten_into(square, flat_ref, tw):
    rows = tw // 8
    step = tw * 8 // 128
    pieces = square.shape[0]
    lane = lax.broadcasted_iota(jnp.int32, (rows, 128), 1)
    total = [None] * step
    for a in range(8):
        first, shift = divmod(a * tw, 128)
        parts = [square[j, pl.ds(a, rows, stride=8), :] for j in range(pieces)]
        if shift:
            parts = [pltpu.roll(x, shift, 1) for x in parts]
        for j in range(pieces + 1):
            if first + j >= step:
                continue
            if not shift:
                if j == pieces:
                    continue
                part = parts[j]
            elif j == 0:
                part = jnp.where(lane >= shift, parts[0], 0.0)
            elif j == pieces:
                part = jnp.where(lane < shift, parts[-1], 0.0)
            else:
                part = jnp.where(lane >= shift, parts[j], parts[j - 1])
            old = total[first + j]
            total[first + j] = part if old is None else old + part
    for i in range(step):
        flat_ref[pl.ds(i, rows, stride=step), :] = total[i]


def gram_kernel(tw, scale, x_ref, flat_ref, square, rowwise):
    x = jnp.concatenate([x_ref[s] for s in range(x_ref.shape[0])], 1)
    width = square.shape[0] * 128
    other = jnp.concatenate([x, jnp.zeros((width - tw, x.shape[1]), x.dtype)], 0)
    full = lax.dot_general(x, other, (((1,), (1,)), ((), ())), preferred_element_type=jnp.float32)
    for j in range(square.shape[0]):
        square[j] = full[:, j * 128 : (j + 1) * 128] * scale
    flatten_into(square, rowwise, tw)
    lines = rowwise.shape[0]
    for i in range(0, lines, 8):
        n = min(8, lines - i)
        flat_ref[0:1, i * 128 : (i + n) * 128] = rowwise[i : i + n, :].reshape(1, n * 128)


def blocked(queries, keys_values, plan, doc_start, keep_blocks, tile_owner):
    rows, width = queries.shape
    devices = lax.axis_size("tokens")
    send = rows // devices
    tw = GROUPS * 2 * BLOCK // devices
    wide = -(-tw // 128) * 128
    span = SPAN * 128
    place = plan // rows * send + plan % send
    pick = (place[None, :] == jnp.arange(rows, dtype=jnp.int32)[:, None]).astype(jnp.bfloat16)
    kv_sorted = jnp.dot(pick, keys_values, preferred_element_type=jnp.float32).astype(jnp.bfloat16)
    starts = (doc_start % rows).astype(jnp.bfloat16)
    extra = jnp.pad(starts[None, :], ((0, PAD - 1), (0, keys_values.shape[1] - rows)))
    gathered = gather(jnp.concatenate([kv_sorted, extra], 0), devices)
    vmem = functools.partial(pl.BlockSpec, memory_space=pltpu.VMEM)
    attended, tiles = pl.pallas_call(
        functools.partial(attention_kernel, devices, tw),
        grid=(PAIRS,),
        in_specs=[
            pl.BlockSpec(memory_space=pltpu.SMEM),
            pl.BlockSpec(memory_space=pltpu.SMEM),
            vmem((1, rows), lambda p: (0, 0)),
            vmem((rows, span), lambda p: (0, p)),
            vmem((devices, rows, 128), lambda p: (0, 0, p)),
            vmem((devices, rows, 128), lambda p: (0, 0, PAIRS + p)),
            vmem((devices, PAD, 128), lambda p: (0, rows // PAD, 0)),
        ],
        out_specs=[
            vmem((rows, span), lambda p: (0, p)),
            vmem((devices, tw, rows), lambda p: (0, 0, 0)),
        ],
        out_shape=[
            jax.ShapeDtypeStruct((rows, width), jnp.bfloat16),
            jax.ShapeDtypeStruct((devices, tw, rows), jnp.bfloat16),
        ],
        scratch_shapes=[
            pltpu.VMEM((SPAN, rows, 128), jnp.float32),
            pltpu.VMEM((devices, rows, 128), jnp.float32),
            pltpu.VMEM((devices, rows, 128), jnp.float32),
            pltpu.VMEM((SPAN, rows, 128), jnp.float32),
            pltpu.VMEM((PAIRS * SPAN, rows, 128), jnp.bfloat16),
            pltpu.SMEM((devices,), jnp.int32),
        ],
        compiler_params=pltpu.CompilerParams(vmem_limit_bytes=50 * 1024 * 1024),
    )(keep_blocks, tile_owner, place[None, :], queries, gathered, gathered, gathered)
    mine = lax.all_to_all(tiles, "tokens", split_axis=0, concat_axis=0, tiled=True)
    flat = pl.pallas_call(
        functools.partial(gram_kernel, tw, 1.0 / (rows * devices)),
        out_shape=jax.ShapeDtypeStruct((1, tw * tw), jnp.float32),
        scratch_shapes=[
            pltpu.VMEM((wide // 128, tw, 128), jnp.float32),
            pltpu.VMEM((tw * tw // 128, 128), jnp.float32),
        ],
        compiler_params=pltpu.CompilerParams(vmem_limit_bytes=40 * 1024 * 1024),
    )(mine)
    return attended, flat


def solution(mesh):
    in_specs = (
        P(("groups", "tokens"), None),
        P(("groups", "tokens"), None),
        P(("groups", "tokens")),
        P(("groups", "tokens")),
        P(),
        P(),
    )
    out_specs = (P(("groups", "tokens"), None), P(("groups", "tokens"), None))
    local = blocked if mesh.shape["tokens"] == 16 else general
    return jax.shard_map(local, mesh=mesh, in_specs=in_specs, out_specs=out_specs, check_vma=False)
```
